512 devices in a mesh: row: 16 (over z_lo, y), col: 4 (over z_hi), rep: 8 (over x, core).
Axes of the slice: x: 4, y: 4, z: 16 (z_hi: 4, z_lo: 4; z = z_hi * 4 + z_lo), core: 2. Of those that a mesh axis runs over, the one named last changes fastest.
Arguments:
- x_t: bfloat16 [128, 65536], P('rep', ('row', 'col')), may hold values from -6 to 6
- weight: bfloat16 [128, 256], replicated, may hold values from -0.5 to 0.5
- cotangent_t: bfloat16 [256, 65536], P('rep', ('row', 'col')), may hold values from -6 to 6
- tile_vals: bfloat16 [16, 4, 96, 128, 128], P('row', 'col'), may hold values from -0.625 to 0.625
- tile_rows: int32 [16, 4, 96], P('row', 'col'), may hold values from 0 to 31, as said below
- tile_cols: int32 [16, 4, 96], P('row', 'col'), may hold values from 0 to 127
- tile_count: int32 [16, 4], P('row', 'col'), may hold values from 1 to 96, as said below
Outputs:
- y_t: bfloat16 [256, 65536], P('rep', ('row', 'col'))
- dx_t: float32 [128, 65536], P('rep', ('row', 'col'))
- weight_grad: float32 [128, 256], P(None, 'rep')
The draws below stay inside these ranges and needn't reach their ends.
Inputs may be any that keep to these rules, and one draw needn't show every extreme that they name: Together with tile_cols at the same index, tile_rows gives within one grid block 96 distinct (row tile, column tile) pairs; entries at t >= tile_count are not part of the graph. `tile_count`: some grid block lists exactly 96 live tiles in every draw.
All inputs are finite; a program needn't handle non-finite values.
Results may differ from the reference program's by a relative error of at most 0.0054.
Values may be sent and summed in bfloat16 or wider, within the bound.
No kernel may reach another device: no remote copies, remote signals or barrier semaphores. Data moves between devices by JAX's collectives and lax.ppermute only.
A program may use at most 64 MiB of HBM per device.

```python
import jax
import jax.numpy as jnp

F_IN = 128
F_OUT = 256
TILE = 128
BT = 8
TILES_DEV = 96
ROW_TILES = 32
COL_TILES = 128
NODES = 65536
N_ROW = 16
N_COL = 4


def tile_slots(key):
    keys = jax.random.split(key, N_ROW * N_COL)
    slots = jax.vmap(lambda k: jax.random.permutation(k, ROW_TILES * COL_TILES)[:TILES_DEV])(keys)
    return slots.reshape(N_ROW, N_COL, TILES_DEV).astype(jnp.int32)


def draw_tile_rows(key, part):
    slots = tile_slots(key)
    return (slots // COL_TILES).astype(jnp.int32)


def draw_tile_cols(key, part):
    slots = tile_slots(key)
    return (slots % COL_TILES).astype(jnp.int32)


def draw_tile_count(key, part):
    key = jax.random.fold_in(key, 3)
    first_key, second_key, pick_key = jax.random.split(key, 3)
    first = jax.random.randint(first_key, (N_ROW * N_COL,), 1, TILES_DEV + 1)
    second = jax.random.randint(second_key, (N_ROW * N_COL,), 1, TILES_DEV + 1)
    counts = jnp.maximum(1, first * second // TILES_DEV)
    chosen = jax.random.randint(pick_key, (), 0, N_ROW * N_COL)
    counts = jnp.where(jnp.arange(N_ROW * N_COL) == chosen, TILES_DEV, counts)
    return counts.reshape(N_ROW, N_COL).astype(jnp.int32)


def levels(rng, shape, shards, smallest, largest):
    def one(dim, shards_of):
        steps = jax.random.uniform(jax.random.fold_in(jax.random.fold_in(rng, 6), dim), (shards_of,), jnp.float32, smallest / len(shards), largest / len(shards))
        return jnp.repeat(jnp.exp(steps), shape[dim] // shards_of).reshape((-1,) + (1,) * (len(shape) - dim - 1))

    loudness = one(*shards[0])
    for cut in shards[1:]:
        loudness = loudness * one(*cut)
    return loudness


def gaussian(own_key, shape, scale, most, cuts=(), held_as=jnp.bfloat16):
    values = jax.random.normal(own_key, shape, jnp.float32) * scale
    if len(cuts) > 0:
        values = levels(own_key, shape, cuts, -0.22, 0.18) * values
    return jnp.clip(values, min=-most, max=most).astype(held_as)


def setup_inputs(seed: int = 0) -> dict:
    key_of = jax.random.split(jax.random.key(seed), 8)
    x_t = gaussian(key_of[0], (F_IN, NODES), 1.0, 6.0, ((0, 8), (1, 64)))
    weight = gaussian(key_of[1], (F_IN, F_OUT), F_IN ** -0.5, 0.5)
    cotangent_t = gaussian(key_of[2], (F_OUT, NODES), 1.0, 6.0, ((0, 8), (1, 64)))
    tile_vals = gaussian(key_of[3], (N_ROW, N_COL, TILES_DEV, TILE, TILE), (0.5 * TILE ** -0.5), 0.625, ((0, 16), (1, 4)))
    tile_rows = draw_tile_rows(jax.random.fold_in(key_of[7], 71), 0)
    tile_cols = draw_tile_cols(jax.random.fold_in(key_of[7], 71), 0)
    tile_count = draw_tile_count(jax.random.fold_in(key_of[7], 71), 0)
    return dict(x_t=x_t, weight=weight, cotangent_t=cotangent_t, tile_vals=tile_vals, tile_rows=tile_rows, tile_cols=tile_cols, tile_count=tile_count)


def reference(x_t, weight, cotangent_t, tile_vals, tile_rows, tile_cols, tile_count):
    n_tiles = NODES // TILE
    x_tiles = x_t.reshape(F_IN, n_tiles, TILE)
    gathered = jnp.zeros((F_IN, n_tiles, TILE), jnp.float32)
    places = []
    for r_at in range(N_ROW):
        for c_at in range(N_COL):
            rows = tile_rows[r_at, c_at].astype(jnp.int32)
            cols = tile_cols[r_at, c_at].astype(jnp.int32)
            global_rows = r_at * ROW_TILES + rows
            global_cols = ((cols // BT) * N_COL + c_at) * BT + cols % BT
            live = (jnp.arange(TILES_DEV, dtype=jnp.int32) < tile_count[r_at, c_at]).astype(jnp.float32)
            values = tile_vals[r_at, c_at].astype(jnp.float32)
            places.append((global_rows, global_cols, live, values))
            picked = x_tiles[:, global_cols].astype(jnp.float32)
            product = jnp.einsum('ftk,tnk->ftn', picked, values) * live[None, :, None]
            gathered = gathered.at[:, global_rows].add(product)
    aggregate_t = gathered.reshape(F_IN, NODES).astype(jnp.bfloat16)
    pre_t = jnp.dot(weight.T, aggregate_t, preferred_element_type=jnp.float32)
    y_t = jax.nn.silu(pre_t).astype(jnp.bfloat16)
    sig = jax.nn.sigmoid(pre_t)
    dpre_t = (cotangent_t.astype(jnp.float32) * sig * (1.0 + pre_t * (1.0 - sig))).astype(jnp.bfloat16)
    weight_grad = jnp.dot(aggregate_t, dpre_t.T, preferred_element_type=jnp.float32)
    dagg_t = jnp.dot(weight, dpre_t, preferred_element_type=jnp.float32).astype(jnp.bfloat16)
    dagg_tiles = dagg_t.reshape(F_IN, n_tiles, TILE)
    back_sum = jnp.zeros((F_IN, n_tiles, TILE), jnp.float32)
    for global_rows, global_cols, live, values in places:
        picked = dagg_tiles[:, global_rows].astype(jnp.float32)
        product = jnp.einsum('ftn,tnk->ftk', picked, values) * live[None, :, None]
        back_sum = back_sum.at[:, global_cols].add(product)
    dx_t = back_sum.reshape(F_IN, NODES)
    return y_t, dx_t, weight_grad
```

```python
import functools

import jax
import jax.numpy as jnp
from jax import lax
from jax.experimental import pallas as pl
from jax.experimental.pallas import tpu as pltpu
from jax.sharding import PartitionSpec as P

BF16 = jnp.bfloat16
F32 = jnp.float32
UNROLL = 8
SMEM = pl.BlockSpec(memory_space=pltpu.SMEM)
VMEM = pl.BlockSpec(memory_space=pltpu.VMEM)
PARAMS = pltpu.CompilerParams(vmem_limit_bytes=32 * 1024 * 1024)


def live_loop(count, body):
    groups = count // UNROLL

    def group(g, carry):
        body(g * UNROLL, UNROLL)
        return carry

    def single(t, carry):
        body(t, 1)
        return carry

    lax.fori_loop(0, groups, group, 0)
    lax.fori_loop(groups * UNROLL, count, single, 0)


def aggregate_kernel(rows, cols, count, x_ref, vals_ref, out_ref, acc):
    acc[...] = jnp.zeros_like(acc)

    def body(first, n):
        products = [
            lax.dot_general(
                x_ref[cols[first + u]],
                vals_ref[first + u],
                (((1,), (1,)), ((), ())),
                preferred_element_type=F32,
            )
            for u in range(n)
        ]
        for u in range(n):
            at = rows[first + u]
            acc[at] = acc[at] + products[u]

    live_loop(count[0], body)
    out_ref[...] = acc[...].astype(out_ref.dtype)


def middle_kernel(h_ref, wt_ref, w_ref, cot_ref, y_ref, terms_ref, grad_ref):
    groups, tiles, feat, tile = h_ref.shape
    wt = wt_ref[...]
    w = w_ref[...]
    grad = jnp.zeros(grad_ref.shape, F32)
    for i in range(tiles):
        at = slice(i * tile, (i + 1) * tile)
        h = h_ref[:, i].reshape(groups * feat, tile)
        pre = jnp.dot(wt, h, preferred_element_type=F32)
        sig = jax.nn.sigmoid(pre)
        y_ref[:, at] = (pre * sig).astype(y_ref.dtype)
        dpre = (cot_ref[:, at].astype(F32) * sig * (1.0 + pre * (1.0 - sig))).astype(BF16)
        terms = jnp.dot(w, dpre, preferred_element_type=F32)
        terms_ref[:, i] = terms.astype(terms_ref.dtype).reshape(groups, feat, tile)
        grad += lax.dot_general(
            dpre, h, (((1,), (1,)), ((), ())), preferred_element_type=F32
        )
    grad_ref[...] = grad


def backward_kernel(rows, cols, count, d_ref, vals_ref, out_ref, acc):
    row_parts, _, tile = out_ref.shape
    feat = acc.shape[1]
    per = acc.shape[0] // row_parts
    slab_rows = per * feat
    acc[...] = jnp.zeros_like(acc)

    def body(first, n):
        products = []
        for u in range(n):
            at = rows[first + u]
            start = pl.multiple_of((at % per) * feat, feat)
            products.append(
                jnp.dot(
                    d_ref[at // per, pl.ds(start, feat), :],
                    vals_ref[first + u],
                    preferred_element_type=F32,
                )
            )
        for u in range(n):
            at = cols[first + u]
            acc[at] = acc[at] + products[u]

    live_loop(count[0], body)
    grad = jnp.sum(d_ref[:, slab_rows:, :].astype(F32), axis=0).astype(out_ref.dtype)
    for r in range(row_parts):
        out_ref[r, :slab_rows, :] = (
            acc[r * per : (r + 1) * per].reshape(slab_rows, tile).astype(out_ref.dtype)
        )
        out_ref[r, slab_rows:, :] = grad


def final_kernel(in_ref, dx_ref, grad_ref):
    feat = dx_ref.shape[0]
    tile = in_ref.shape[2]
    slab_rows = in_ref.shape[1] - grad_ref.shape[0]
    for i in range(slab_rows // feat):
        dx_ref[:, i * tile : (i + 1) * tile] = jnp.sum(
            in_ref[:, i * feat : (i + 1) * feat, :].astype(F32), axis=0
        )
    grad_ref[...] = jnp.sum(in_ref[:, slab_rows:, :].astype(F32), axis=0)


def exchange(parts, axis):
    return lax.all_to_all(parts, axis, 0, 0, tiled=True)


def local(x_t, weight, cotangent_t, tile_vals, tile_rows, tile_cols, tile_count):
    feat, slab = x_t.shape
    tile = tile_vals.shape[-1]
    per = slab // tile
    n_row, n_col, n_rep = lax.axis_size("row"), lax.axis_size("col"), lax.axis_size("rep")
    values = tile_vals[0, 0]
    rows = tile_rows[0, 0]
    cols = tile_cols[0, 0]
    count = tile_count[0]
    out_loc = weight.shape[1] // n_rep
    w_cols = lax.dynamic_slice_in_dim(weight, lax.axis_index("rep") * out_loc, out_loc, 1)

    x_tiles = x_t.reshape(feat, per, tile).transpose(1, 0, 2)
    x_all = exchange(jnp.broadcast_to(x_tiles[None], (n_row, per, feat, tile)), "row")

    part = pl.pallas_call(
        aggregate_kernel,
        out_shape=jax.ShapeDtypeStruct((n_col * per, feat, tile), BF16),
        in_specs=[SMEM, SMEM, SMEM, VMEM, VMEM],
        out_specs=VMEM,
        scratch_shapes=[pltpu.VMEM((n_col * per, feat, tile), F32)],
        compiler_params=PARAMS,
        name="aggregate",
    )(rows, cols, count, x_all.reshape(n_row * per, feat, tile), values)

    part = exchange(part.reshape(n_col, per, feat, tile), "col")
    mine = jnp.sum(part.astype(F32), axis=0).astype(BF16)
    h_all = exchange(jnp.broadcast_to(mine[None], (n_rep, per, feat, tile)), "rep")

    y, terms, grad = pl.pallas_call(
        middle_kernel,
        out_shape=(
            jax.ShapeDtypeStruct((out_loc, slab), BF16),
            jax.ShapeDtypeStruct((n_rep, per, feat, tile), BF16),
            jax.ShapeDtypeStruct((out_loc, n_rep * feat), F32),
        ),
        in_specs=[VMEM] * 4,
        out_specs=(VMEM, VMEM, VMEM),
        compiler_params=PARAMS,
        name="middle",
    )(h_all, w_cols.T, w_cols, cotangent_t)

    terms = exchange(terms, "rep")
    dagg = jnp.sum(terms.astype(F32), axis=0).astype(BF16)
    grad_rows = out_loc * n_rep * feat // tile
    send = jnp.concatenate(
        [dagg.reshape(per * feat, tile), grad.reshape(grad_rows, tile).astype(BF16)], axis=0
    )
    d_all = exchange(jnp.broadcast_to(send[None], (n_col,) + send.shape), "col")

    back = pl.pallas_call(
        backward_kernel,
        out_shape=jax.ShapeDtypeStruct((n_row,) + send.shape, BF16),
        in_specs=[SMEM, SMEM, SMEM, VMEM, VMEM],
        out_specs=VMEM,
        scratch_shapes=[pltpu.VMEM((n_row * per, feat, tile), F32)],
        compiler_params=PARAMS,
        name="backward",
    )(rows, cols, count, d_all, values)
    back = exchange(back, "row")

    dx, grad = pl.pallas_call(
        final_kernel,
        out_shape=(
            jax.ShapeDtypeStruct((feat, slab), F32),
            jax.ShapeDtypeStruct((grad_rows, tile), F32),
        ),
        in_specs=[VMEM],
        out_specs=(VMEM, VMEM),
        compiler_params=PARAMS,
        name="final",
    )(back)
    return y, dx, grad.reshape(out_loc, n_rep * feat).T


def solution(mesh):
    return jax.shard_map(
        local,
        mesh=mesh,
        in_specs=(
            P("rep", ("row", "col")),
            P(),
            P("rep", ("row", "col")),
            P("row", "col", None, None, None),
            P("row", "col", None),
            P("row", "col", None),
            P("row", "col"),
        ),
        out_specs=(P("rep", ("row", "col")), P("rep", ("row", "col")), P(None, "rep")),
        check_vma=False,
    )
```

```python
import jax
import jax.numpy as jnp
from jax import lax
from jax.experimental import pallas as pl
from jax.experimental.pallas import tpu as pltpu
from jax.sharding import PartitionSpec as P

BF16 = jnp.bfloat16
F32 = jnp.float32
UNROLL = 32
SMEM = pl.BlockSpec(memory_space=pltpu.SMEM)
VMEM = pl.BlockSpec(memory_space=pltpu.VMEM)
HBM = pl.BlockSpec(memory_space=pltpu.HBM)
PARAMS = pltpu.CompilerParams(vmem_limit_bytes=24 * 1024 * 1024)


def call(kernel, out, in_specs, name, scratch=()):
    return pl.pallas_call(
        kernel,
        out_shape=out,
        in_specs=in_specs,
        out_specs=jax.tree.map(lambda _: VMEM, out),
        scratch_shapes=list(scratch),
        compiler_params=PARAMS,
        name=name,
    )


def copies_kernel(x_ref, out_ref):
    for r in range(out_ref.shape[0]):
        out_ref[r] = x_ref[...]


def stage_kernel(vals_hbm, w_in, cot_in, vals_ref, wt_ref, parts_ref, sems):
    n = sems.shape[0]
    per = vals_ref.shape[0] // n
    copies = [
        pltpu.make_async_copy(
            vals_hbm.at[pl.ds(i * per, per)], vals_ref.at[pl.ds(i * per, per)], sems.at[i]
        )
        for i in range(n)
    ]
    for copy in copies:
        copy.start()
    wt_ref[...] = w_in[...].astype(F32).T.astype(wt_ref.dtype)
    tile = parts_ref.shape[2]
    for i in range(parts_ref.shape[0]):
        parts_ref[i] = cot_in[:, i * tile : (i + 1) * tile]
    for copy in copies:
        copy.wait()


def live_loop(count, products, add):
    def group(g, carry):
        first = g * UNROLL
        found = [products(first + u) for u in range(UNROLL)]
        for u in range(UNROLL):
            add(first + u, jnp.where(first + u < count, found[u], 0.0))
        return carry

    lax.fori_loop(0, (count + UNROLL - 1) // UNROLL, group, 0)


def aggregate_kernel(meta, x_ref, vals_ref, out_ref, acc):
    listed, tile = vals_ref.shape[:2]
    per = x_ref.shape[2] // tile
    acc[...] = jnp.zeros_like(acc)

    def product(t):
        at = meta[listed + t]
        start = pl.multiple_of((at % per) * tile, tile)
        return lax.dot_general(
            x_ref[at // per, :, pl.ds(start, tile)],
            vals_ref[t],
            (((1,), (1,)), ((), ())),
            preferred_element_type=F32,
        )

    def add(t, found):
        acc[meta[t]] = acc[meta[t]] + found

    live_loop(meta[2 * listed], product, add)
    out_ref[...] = acc[...].astype(out_ref.dtype)


def spread_kernel(part_ref, out_ref):
    total = jnp.sum(part_ref[...].astype(F32), axis=0).astype(out_ref.dtype)
    for i in range(out_ref.shape[0]):
        out_ref[i] = total


def middle_kernel(meta, h_ref, wt_ref, cot_ref, y_ref, terms_ref, grad_ref):
    groups, rows, tile = h_ref.shape
    tiles, outs = cot_ref.shape[:2]
    feat = rows // tiles
    wt = wt_ref[pl.ds(pl.multiple_of(meta[meta.shape[0] - 1] * outs, outs), outs), :]
    grad = jnp.zeros(grad_ref.shape, F32)
    for i in range(tiles):
        at = slice(i * tile, (i + 1) * tile)
        rows_at = slice(i * feat, (i + 1) * feat)
        h = h_ref[:, rows_at, :].reshape(groups * feat, tile)
        pre = jnp.dot(wt, h, preferred_element_type=F32)
        sig = jax.nn.sigmoid(pre)
        y_ref[:, at] = (pre * sig).astype(y_ref.dtype)
        dpre = (cot_ref[i].astype(F32) * sig * (1.0 + pre * (1.0 - sig))).astype(BF16)
        terms = lax.dot_general(
            wt, dpre, (((0,), (0,)), ((), ())), preferred_element_type=F32
        )
        terms_ref[:, rows_at, :] = terms.astype(terms_ref.dtype).reshape(groups, feat, tile)
        grad += lax.dot_general(
            dpre, h, (((1,), (1,)), ((), ())), preferred_element_type=F32
        )
    grad_ref[...] = grad.astype(grad_ref.dtype)


def pack_kernel(terms_ref, grad_ref, out_ref):
    total = jnp.sum(terms_ref[...].astype(F32), axis=0).astype(out_ref.dtype)
    rows = total.shape[0]
    for i in range(out_ref.shape[0]):
        out_ref[i, :rows] = total
        out_ref[i, rows:] = grad_ref[...]


def backward_kernel(meta, d_ref, vals_ref, out_ref, acc):
    listed = vals_ref.shape[0]
    parts, rows, tile = out_ref.shape
    per = acc.shape[0] // parts
    feat = acc.shape[1]
    slab_rows = per * feat
    acc[...] = jnp.zeros_like(acc)

    def product(t):
        at = meta[t]
        start = pl.multiple_of((at % per) * feat, feat)
        return jnp.dot(
            d_ref[at // per, pl.ds(start, feat), :], vals_ref[t], preferred_element_type=F32
        )

    def add(t, found):
        at = meta[listed + t]
        acc[at] = acc[at] + found

    live_loop(meta[2 * listed], product, add)
    grad = jnp.sum(d_ref[:, slab_rows:, :].astype(F32), axis=0).astype(out_ref.dtype)
    for r in range(parts):
        out_ref[r, :slab_rows] = (
            acc[r * per : (r + 1) * per].reshape(slab_rows, tile).astype(out_ref.dtype)
        )
        out_ref[r, slab_rows:] = grad


def final_kernel(in_ref, dx_ref, grad_ref):
    feat = dx_ref.shape[0]
    tile = in_ref.shape[2]
    slab_rows = in_ref.shape[1] - grad_ref.shape[0]
    for i in range(slab_rows // feat):
        dx_ref[:, i * tile : (i + 1) * tile] = jnp.sum(
            in_ref[:, i * feat : (i + 1) * feat, :].astype(F32), axis=0
        )
    grad_ref[...] = jnp.sum(in_ref[:, slab_rows:, :].astype(F32), axis=0)


def exchange(parts, axis):
    return lax.all_to_all(parts, axis, 0, 0, tiled=True)


def local(x_t, weight, cotangent_t, tile_vals, tile_rows, tile_cols, tile_count):
    feat, slab = x_t.shape
    tile = tile_vals.shape[-1]
    listed = tile_vals.shape[2]
    per = slab // tile
    n_row, n_col, n_rep = lax.axis_size("row"), lax.axis_size("col"), lax.axis_size("rep")
    rep_at = lax.axis_index("rep")
    out_loc = weight.shape[1] // n_rep
    grad_shape = (out_loc, n_rep * feat)
    shape = jax.ShapeDtypeStruct

    meta = jnp.concatenate(
        [tile_rows[0, 0], tile_cols[0, 0], tile_count[0], rep_at.reshape(1)]
    )

    x_parts = call(copies_kernel, shape((n_row, feat, slab), BF16), [VMEM], "copies")(x_t)
    x_all = exchange(x_parts, "row")
    vals, wt, cot = call(
        stage_kernel,
        (
            shape((listed, tile, tile), BF16),
            shape(weight.shape[::-1], BF16),
            shape((n_rep, out_loc, tile), BF16),
        ),
        [HBM, VMEM, VMEM],
        "stage",
        [pltpu.SemaphoreType.DMA((8,))],
    )(tile_vals[0, 0], weight, cotangent_t)

    part = call(
        aggregate_kernel,
        shape((n_col * per, feat, tile), BF16),
        [SMEM, VMEM, VMEM],
        "aggregate",
        [pltpu.VMEM((n_col * per, feat, tile), F32)],
    )(meta, x_all, vals)
    part = exchange(part.reshape(n_col, per * feat, tile), "col")

    mine = call(spread_kernel, shape((n_rep, per * feat, tile), BF16), [VMEM], "spread")(part)
    h_all = exchange(mine, "rep")

    y, terms, grad = call(
        middle_kernel,
        (
            shape((out_loc, slab), BF16),
            shape((n_rep, per * feat, tile), BF16),
            shape(grad_shape, BF16),
        ),
        [SMEM, VMEM, VMEM, VMEM],
        "middle",
    )(meta, h_all, wt, cot)
    terms = exchange(terms, "rep")
    send = call(
        pack_kernel, shape((n_col, per * feat + out_loc, tile), BF16), [VMEM, VMEM], "pack"
    )(terms, grad)
    d_all = exchange(send, "col")

    back = call(
        backward_kernel,
        shape((n_row, per * feat + out_loc, tile), BF16),
        [SMEM, VMEM, VMEM],
        "backward",
        [pltpu.VMEM((n_row * per, feat, tile), F32)],
    )(meta, d_all, vals)
    back = exchange(back, "row")

    dx, grad = call(
        final_kernel, (shape((feat, slab), F32), shape(grad_shape, F32)), [VMEM], "final"
    )(back)
    return y, dx, grad.T


def solution(mesh):
    return jax.shard_map(
        local,
        mesh=mesh,
        in_specs=(
            P("rep", ("row", "col")),
            P(),
            P("rep", ("row", "col")),
            P("row", "col", None, None, None),
            P("row", "col", None),
            P("row", "col", None),
            P("row", "col"),
        ),
        out_specs=(P("rep", ("row", "col")), P("rep", ("row", "col")), P(None, "rep")),
        check_vma=False,
    )
```

```python
import jax
import jax.numpy as jnp
from jax import lax
from jax.experimental import pallas as pl
from jax.experimental.pallas import tpu as pltpu
from jax.sharding import PartitionSpec as P

BF16 = jnp.bfloat16
F32 = jnp.float32
UNROLL = 32
SMEM = pl.BlockSpec(memory_space=pltpu.SMEM)
VMEM = pl.BlockSpec(memory_space=pltpu.VMEM)
HBM = pl.BlockSpec(memory_space=pltpu.HBM)
PARAMS = pltpu.CompilerParams(vmem_limit_bytes=24 * 1024 * 1024)


def call(kernel, out, in_specs, name, scratch=()):
    return pl.pallas_call(
        kernel,
        out_shape=out,
        in_specs=in_specs,
        out_specs=jax.tree.map(lambda _: VMEM, out),
        scratch_shapes=list(scratch),
        compiler_params=PARAMS,
        name=name,
    )


def copies_kernel(x_ref, out_ref):
    for r in range(out_ref.shape[0]):
        out_ref[r] = x_ref[...]


def stage_kernel(vals_hbm, vals_ref, sems):
    n = sems.shape[0]
    per = vals_ref.shape[0] // n
    copies = [
        pltpu.make_async_copy(
            vals_hbm.at[pl.ds(i * per, per)], vals_ref.at[pl.ds(i * per, per)], sems.at[i]
        )
        for i in range(n)
    ]
    for copy in copies:
        copy.start()
    for copy in copies:
        copy.wait()


def cut_kernel(cot_ref, keep_ref, send_ref):
    tile = keep_ref.shape[2]
    me = lax.axis_index("rep")
    for k in range(2 * keep_ref.shape[0]):
        out_ref = send_ref if k % 2 else keep_ref
        start = pl.multiple_of((me ^ k) * tile, tile)
        out_ref[k // 2] = cot_ref[:, pl.ds(start, tile)]


def live_loop(count, products, add):
    def group(g, carry):
        first = g * UNROLL
        found = [products(first + u) for u in range(UNROLL)]
        for u in range(UNROLL):
            add(first + u, jnp.where(first + u < count, found[u], 0.0))
        return carry

    lax.fori_loop(0, (count + UNROLL - 1) // UNROLL, group, 0)


def aggregate_kernel(meta, x_ref, vals_ref, out_ref, acc):
    listed, tile = vals_ref.shape[:2]
    per = x_ref.shape[2] // tile
    acc[...] = jnp.zeros_like(acc)

    def product(t):
        at = meta[listed + t]
        start = pl.multiple_of((at % per) * tile, tile)
        return lax.dot_general(
            x_ref[at // per, :, pl.ds(start, tile)],
            vals_ref[t],
            (((1,), (1,)), ((), ())),
            preferred_element_type=F32,
        )

    def add(t, found):
        acc[meta[t]] = acc[meta[t]] + found

    live_loop(meta[2 * listed], product, add)
    out_ref[...] = acc[...].astype(out_ref.dtype)


def tile_kernel(part_ref, w_ref, low_ref, high_ref, out_ref, cot_all):
    groups, _, tile = out_ref.shape
    feat = part_ref.shape[1]
    half, outs = low_ref.shape[:2]
    me = lax.axis_index("rep")
    for k in range(groups):
        cot_all[me ^ k] = low_ref[k] if k < half else high_ref[k - half]
    h = jnp.sum(
        part_ref[...].reshape(-1, groups * feat, tile).astype(F32), axis=0
    ).astype(BF16)
    w = w_ref[...]
    pre = lax.dot_general(w, h, (((0,), (0,)), ((), ())), preferred_element_type=F32)
    sig = jax.nn.sigmoid(pre)
    cot = cot_all[...].reshape(groups * outs, tile).astype(F32)
    dpre = (cot * sig * (1.0 + pre * (1.0 - sig))).astype(BF16)
    dagg = jnp.dot(w, dpre, preferred_element_type=F32)
    grad = lax.dot_general(dpre, h, (((1,), (1,)), ((), ())), preferred_element_type=F32)
    y = pre * sig
    dtype = out_ref.dtype
    out_ref[:, :feat] = dagg.astype(dtype).reshape(groups, feat, tile)
    out_ref[:, feat : feat + outs] = y.astype(dtype).reshape(groups, outs, tile)
    out_ref[:, feat + outs :] = grad.astype(dtype).reshape(groups, outs, tile)


def pack_kernel(in_ref, out_ref):
    tiles, in_rows, tile = in_ref.shape
    outs = (in_rows * tiles - out_ref.shape[1]) // (2 * tiles - 1)
    feat = in_rows - 2 * outs
    rows = tiles * feat
    dagg = in_ref[:, :feat].reshape(rows, tile)
    grad = jnp.sum(in_ref[:, feat + outs :].astype(F32), axis=0).astype(out_ref.dtype)
    for i in range(out_ref.shape[0]):
        out_ref[i, :rows] = dagg
        out_ref[i, rows:] = grad


def backward_kernel(meta, d_ref, vals_ref, out_ref, acc):
    listed = vals_ref.shape[0]
    parts, rows, tile = out_ref.shape
    per = acc.shape[0] // parts
    feat = acc.shape[1]
    slab_rows = per * feat
    acc[...] = jnp.zeros_like(acc)

    def product(t):
        at = meta[t]
        start = pl.multiple_of((at % per) * feat, feat)
        return jnp.dot(
            d_ref[at // per, pl.ds(start, feat), :], vals_ref[t], preferred_element_type=F32
        )

    def add(t, found):
        at = meta[listed + t]
        acc[at] = acc[at] + found

    live_loop(meta[2 * listed], product, add)
    grad = jnp.sum(d_ref[:, slab_rows:, :].astype(F32), axis=0).astype(out_ref.dtype)
    for r in range(parts):
        out_ref[r, :slab_rows] = (
            acc[r * per : (r + 1) * per].reshape(slab_rows, tile).astype(out_ref.dtype)
        )
        out_ref[r, slab_rows:] = grad


def final_kernel(in_ref, mid_ref, dx_ref, y_ref, grad_ref):
    feat = dx_ref.shape[0]
    tile = in_ref.shape[2]
    slab_rows = in_ref.shape[1] - grad_ref.shape[0]
    for i in range(slab_rows // feat):
        dx_ref[:, i * tile : (i + 1) * tile] = jnp.sum(
            in_ref[:, i * feat : (i + 1) * feat, :].astype(F32), axis=0
        )
    grad_ref[...] = jnp.sum(in_ref[:, slab_rows:, :].astype(F32), axis=0)
    outs = y_ref.shape[0]
    for i in range(mid_ref.shape[0]):
        y_ref[:, i * tile : (i + 1) * tile] = mid_ref[i, feat : feat + outs]


def exchange(parts, axis):
    return lax.all_to_all(parts, axis, 0, 0, tiled=True)


def swap(parts, bit):
    n = lax.axis_size("rep")
    return lax.ppermute(parts, "rep", [(i, i ^ bit) for i in range(n)])


def local(x_t, weight, cotangent_t, tile_vals, tile_rows, tile_cols, tile_count):
    feat, slab = x_t.shape
    tile = tile_vals.shape[-1]
    listed = tile_vals.shape[2]
    per = slab // tile
    n_row, n_col, n_rep = lax.axis_size("row"), lax.axis_size("col"), lax.axis_size("rep")
    out_loc = weight.shape[1] // n_rep
    grad_shape = (out_loc, n_rep * feat)
    shape = jax.ShapeDtypeStruct

    meta = jnp.concatenate([tile_rows[0, 0], tile_cols[0, 0], tile_count[0]])

    x_parts = call(copies_kernel, shape((n_row, feat, slab), BF16), [VMEM], "copies")(x_t)
    x_all = exchange(x_parts, "row")
    half = shape((n_rep // 2, out_loc, tile), BF16)
    keep, send = call(cut_kernel, (half, half), [VMEM], "cut")(cotangent_t)
    got = swap(send, 1)
    keep, send = (
        jnp.stack([keep[i], got[i], keep[i + 2], got[i + 2]]) for i in range(2)
    )
    got = swap(send, 2)
    keep, send = (
        jnp.stack([keep[i], keep[i + 1], got[i], got[i + 1]]) for i in (0, 2)
    )
    x_all, keep, send = lax.optimization_barrier((x_all, keep, send))
    got = swap(send, 4)
    vals = call(
        stage_kernel,
        shape((listed, tile, tile), BF16),
        [HBM],
        "stage",
        [pltpu.SemaphoreType.DMA((8,))],
    )(tile_vals[0, 0])

    part = call(
        aggregate_kernel,
        shape((n_col * per, feat, tile), BF16),
        [SMEM, VMEM, VMEM],
        "aggregate",
        [pltpu.VMEM((n_col * per, feat, tile), F32)],
    )(meta, x_all, vals)
    part = exchange(part, ("col", "rep"))

    mid_rows = feat + 2 * out_loc
    mid = call(
        tile_kernel,
        shape((n_rep, mid_rows, tile), BF16),
        [VMEM] * 4,
        "tile",
        [pltpu.VMEM((n_rep, out_loc, tile), BF16)],
    )(part, weight, keep, got)
    mid = exchange(mid, "rep")
    send = call(pack_kernel, shape((n_col, per * feat + out_loc, tile), BF16), [VMEM], "pack")(mid)
    d_all = exchange(send, "col")

    back = call(
        backward_kernel,
        shape((n_row, per * feat + out_loc, tile), BF16),
        [SMEM, VMEM, VMEM],
        "backward",
        [pltpu.VMEM((n_row * per, feat, tile), F32)],
    )(meta, d_all, vals)
    back = exchange(back, "row")

    dx, y, grad = call(
        final_kernel,
        (shape((feat, slab), F32), shape((out_loc, slab), BF16), shape(grad_shape, F32)),
        [VMEM, VMEM],
        "final",
    )(back, mid)
    return y, dx, grad.T


def solution(mesh):
    return jax.shard_map(
        local,
        mesh=mesh,
        in_specs=(
            P("rep", ("row", "col")),
            P(),
            P("rep", ("row", "col")),
            P("row", "col", None, None, None),
            P("row", "col", None),
            P("row", "col", None),
            P("row", "col"),
        ),
        out_specs=(P("rep", ("row", "col")), P("rep", ("row", "col")), P(None, "rep")),
        check_vma=False,
    )
```

```python
import functools

import jax
import jax.numpy as jnp
from jax import lax
from jax.experimental import pallas as pl
from jax.experimental.pallas import tpu as pltpu
from jax.sharding import PartitionSpec as P

BF16 = jnp.bfloat16
F32 = jnp.float32
UNROLL = 32
SMEM = pl.BlockSpec(memory_space=pltpu.SMEM)
VMEM = pl.BlockSpec(memory_space=pltpu.VMEM)
HBM = pl.BlockSpec(memory_space=pltpu.HBM)
PARAMS = pltpu.CompilerParams(vmem_limit_bytes=24 * 1024 * 1024)


def call(kernel, out, in_specs, name, scratch=()):
    return pl.pallas_call(
        kernel,
        out_shape=out,
        in_specs=in_specs,
        out_specs=jax.tree.map(lambda _: VMEM, out),
        scratch_shapes=list(scratch),
        compiler_params=PARAMS,
        name=name,
    )


def copies_kernel(x_ref, out_ref):
    for r in range(out_ref.shape[0]):
        out_ref[r] = x_ref[...]


def stage_kernel(vals_hbm, vals_ref, sems):
    n = sems.shape[0]
    per = vals_ref.shape[0] // n
    copies = [
        pltpu.make_async_copy(
            vals_hbm.at[pl.ds(i * per, per)], vals_ref.at[pl.ds(i * per, per)], sems.at[i]
        )
        for i in range(n)
    ]
    for copy in copies:
        copy.start()
    for copy in copies:
        copy.wait()


def cut_kernel(cot_ref, keep_ref, send_ref):
    tile = keep_ref.shape[2]
    me = lax.axis_index("rep")
    for k in range(2 * keep_ref.shape[0]):
        out_ref = send_ref if k % 2 else keep_ref
        start = pl.multiple_of((me ^ k) * tile, tile)
        out_ref[k // 2] = cot_ref[:, pl.ds(start, tile)]


def live_loop(count, products, add):
    def group(g, carry):
        first = g * UNROLL
        found = [products(first + u) for u in range(UNROLL)]
        for u in range(UNROLL):
            add(first + u, jnp.where(first + u < count, found[u], 0.0))
        return carry

    lax.fori_loop(0, (count + UNROLL - 1) // UNROLL, group, 0)


def aggregate_kernel(row_turn, turn, meta, x_ref, vals_ref, out_ref, acc):
    listed, tile = vals_ref.shape[:2]
    per = x_ref.shape[2] // tile
    acc[...] = jnp.zeros_like(acc)

    def product(t):
        at = meta[listed + t]
        start = pl.multiple_of((at % per) * tile, tile)
        return lax.dot_general(
            x_ref[turned_at(at // per, row_turn, x_ref.shape[0]), :, pl.ds(start, tile)],
            vals_ref[t],
            (((1,), (1,)), ((), ())),
            preferred_element_type=F32,
        )

    def add(t, found):
        acc[meta[t]] = acc[meta[t]] + found

    live_loop(meta[2 * listed], product, add)
    cut = turn * per
    out_ref[: acc.shape[0] - cut] = acc[cut:].astype(out_ref.dtype)
    out_ref[acc.shape[0] - cut :] = acc[:cut].astype(out_ref.dtype)


def tile_kernel(part_ref, w_ref, low_ref, high_ref, out_ref, cot_all):
    groups, _, tile = out_ref.shape
    feat = part_ref.shape[1]
    half, outs = low_ref.shape[:2]
    me = lax.axis_index("rep")
    for k in range(groups):
        cot_all[me ^ k] = low_ref[k] if k < half else high_ref[k - half]
    h = jnp.sum(
        part_ref[...].reshape(-1, groups * feat, tile).astype(F32), axis=0
    ).astype(BF16)
    w = w_ref[...]
    pre = lax.dot_general(w, h, (((0,), (0,)), ((), ())), preferred_element_type=F32)
    sig = jax.nn.sigmoid(pre)
    cot = cot_all[...].reshape(groups * outs, tile).astype(F32)
    dpre = (cot * sig * (1.0 + pre * (1.0 - sig))).astype(BF16)
    dagg = jnp.dot(w, dpre, preferred_element_type=F32)
    grad = lax.dot_general(dpre, h, (((1,), (1,)), ((), ())), preferred_element_type=F32)
    y = pre * sig
    dtype = out_ref.dtype
    out_ref[:, :feat] = dagg.astype(dtype).reshape(groups, feat, tile)
    out_ref[:, feat : feat + outs] = y.astype(dtype).reshape(groups, outs, tile)
    out_ref[:, feat + outs :] = grad.astype(dtype).reshape(groups, outs, tile)


def pack_kernel(in_ref, out_ref):
    tiles, in_rows, tile = in_ref.shape
    outs = (in_rows * tiles - out_ref.shape[1]) // (2 * tiles - 1)
    feat = in_rows - 2 * outs
    rows = tiles * feat
    dagg = in_ref[:, :feat].reshape(rows, tile)
    grad = jnp.sum(in_ref[:, feat + outs :].astype(F32), axis=0).astype(out_ref.dtype)
    for i in range(out_ref.shape[0]):
        out_ref[i, :rows] = dagg
        out_ref[i, rows:] = grad


def backward_kernel(row_turn, turn, meta, d_ref, vals_ref, out_ref, acc):
    listed = vals_ref.shape[0]
    parts, rows, tile = out_ref.shape
    per = acc.shape[0] // parts
    feat = acc.shape[1]
    slab_rows = per * feat
    acc[...] = jnp.zeros_like(acc)

    def product(t):
        at = meta[t]
        start = pl.multiple_of((at % per) * feat, feat)
        return jnp.dot(
            d_ref[turned_at(at // per, turn, d_ref.shape[0]), pl.ds(start, feat), :],
            vals_ref[t],
            preferred_element_type=F32,
        )

    def add(t, found):
        at = meta[listed + t]
        acc[at] = acc[at] + found

    live_loop(meta[2 * listed], product, add)
    grad = jnp.sum(d_ref[:, slab_rows:, :].astype(F32), axis=0).astype(out_ref.dtype)
    for i in range(parts):
        r = (i + row_turn) % parts
        out_ref[i, :slab_rows] = (
            acc[r * per : (r + 1) * per].reshape(slab_rows, tile).astype(out_ref.dtype)
        )
        out_ref[i, slab_rows:] = grad


def final_kernel(in_ref, mid_ref, dx_ref, y_ref, grad_ref):
    feat = dx_ref.shape[0]
    tile = in_ref.shape[2]
    slab_rows = in_ref.shape[1] - grad_ref.shape[0]
    for i in range(slab_rows // feat):
        dx_ref[:, i * tile : (i + 1) * tile] = jnp.sum(
            in_ref[:, i * feat : (i + 1) * feat, :].astype(F32), axis=0
        )
    grad_ref[...] = jnp.sum(in_ref[:, slab_rows:, :].astype(F32), axis=0)
    outs = y_ref.shape[0]
    for i in range(mid_ref.shape[0]):
        y_ref[:, i * tile : (i + 1) * tile] = mid_ref[i, feat : feat + outs]


def turned_at(member, turn, n):
    return (member + n - turn) % n


def exchange(parts, axis, turn=0):
    n = lax.axis_size(axis)
    groups = [[(i + turn) % n for i in range(n)]] if turn else None
    return lax.all_to_all(parts, axis, 0, 0, axis_index_groups=groups, tiled=True)


def swap(parts, bit):
    n = lax.axis_size("rep")
    return lax.ppermute(parts, "rep", [(i, i ^ bit) for i in range(n)])


def local(x_t, weight, cotangent_t, tile_vals, tile_rows, tile_cols, tile_count):
    feat, slab = x_t.shape
    tile = tile_vals.shape[-1]
    listed = tile_vals.shape[2]
    per = slab // tile
    n_row, n_col, n_rep = lax.axis_size("row"), lax.axis_size("col"), lax.axis_size("rep")
    out_loc = weight.shape[1] // n_rep
    row_turn, col_turn = n_row // 4, n_col // 2
    grad_shape = (out_loc, n_rep * feat)
    shape = jax.ShapeDtypeStruct

    meta = jnp.concatenate([tile_rows[0, 0], tile_cols[0, 0], tile_count[0]])

    x_parts = call(copies_kernel, shape((n_row, feat, slab), BF16), [VMEM], "copies")(x_t)
    x_all = exchange(x_parts, "row", row_turn)
    half = shape((n_rep // 2, out_loc, tile), BF16)
    keep, send = call(cut_kernel, (half, half), [VMEM], "cut")(cotangent_t)
    got = swap(send, 1)
    keep, send = (
        jnp.stack([keep[i], got[i], keep[i + 2], got[i + 2]]) for i in range(2)
    )
    got = swap(send, 2)
    keep, send = (
        jnp.stack([keep[i], keep[i + 1], got[i], got[i + 1]]) for i in (0, 2)
    )
    x_all, keep, send = lax.optimization_barrier((x_all, keep, send))
    got = swap(send, 4)
    vals = call(
        stage_kernel,
        shape((listed, tile, tile), BF16),
        [HBM],
        "stage",
        [pltpu.SemaphoreType.DMA((8,))],
    )(tile_vals[0, 0])

    part = call(
        functools.partial(aggregate_kernel, row_turn, col_turn),
        shape((n_col * per, feat, tile), BF16),
        [SMEM, VMEM, VMEM],
        "aggregate",
        [pltpu.VMEM((n_col * per, feat, tile), F32)],
    )(meta, x_all, vals)
    part = exchange(part, ("col", "rep"), col_turn * n_rep)

    mid_rows = feat + 2 * out_loc
    mid = call(
        tile_kernel,
        shape((n_rep, mid_rows, tile), BF16),
        [VMEM] * 4,
        "tile",
        [pltpu.VMEM((n_rep, out_loc, tile), BF16)],
    )(part, weight, keep, got)
    mid = exchange(mid, "rep")
    send = call(pack_kernel, shape((n_col, per * feat + out_loc, tile), BF16), [VMEM], "pack")(mid)
    d_all = exchange(send, "col", col_turn)

    back = call(
        functools.partial(backward_kernel, row_turn, col_turn),
        shape((n_row, per * feat + out_loc, tile), BF16),
        [SMEM, VMEM, VMEM],
        "backward",
        [pltpu.VMEM((n_row * per, feat, tile), F32)],
    )(meta, d_all, vals)
    back = exchange(back, "row", row_turn)

    dx, y, grad = call(
        final_kernel,
        (shape((feat, slab), F32), shape((out_loc, slab), BF16), shape(grad_shape, F32)),
        [VMEM, VMEM],
        "final",
    )(back, mid)
    return y, dx, grad.T


def solution(mesh):
    return jax.shard_map(
        local,
        mesh=mesh,
        in_specs=(
            P("rep", ("row", "col")),
            P(),
            P("rep", ("row", "col")),
            P("row", "col", None, None, None),
            P("row", "col", None),
            P("row", "col", None),
            P("row", "col"),
        ),
        out_specs=(P("rep", ("row", "col")), P("rep", ("row", "col")), P(None, "rep")),
        check_vma=False,
    )
```

```python
import functools

import jax
import jax.numpy as jnp
from jax import lax
from jax.experimental import pallas as pl
from jax.experimental.pallas import tpu as pltpu
from jax.sharding import PartitionSpec as P

BF16 = jnp.bfloat16
F32 = jnp.float32
UNROLL = 32
SMEM = pl.BlockSpec(memory_space=pltpu.SMEM)
VMEM = pl.BlockSpec(memory_space=pltpu.VMEM)
HBM = pl.BlockSpec(memory_space=pltpu.HBM)
PARAMS = pltpu.CompilerParams(vmem_limit_bytes=24 * 1024 * 1024)


def call(kernel, out, in_specs, name, scratch=()):
    return pl.pallas_call(
        kernel,
        out_shape=out,
        in_specs=in_specs,
        out_specs=jax.tree.map(lambda _: VMEM, out),
        scratch_shapes=list(scratch),
        compiler_params=PARAMS,
        name=name,
    )


def copies_kernel(x_ref, out_ref):
    for r in range(out_ref.shape[0]):
        out_ref[r] = x_ref[...]


def stage_kernel(vals_hbm, vals_ref, sems):
    n = sems.shape[0]
    per = vals_ref.shape[0] // n
    copies = [
        pltpu.make_async_copy(
            vals_hbm.at[pl.ds(i * per, per)], vals_ref.at[pl.ds(i * per, per)], sems.at[i]
        )
        for i in range(n)
    ]
    for copy in copies:
        copy.start()
    for copy in copies:
        copy.wait()


def cut_kernel(cot_ref, keep_ref, send_ref):
    tile = keep_ref.shape[2]
    me = lax.axis_index("rep")
    for k in range(2 * keep_ref.shape[0]):
        out_ref = send_ref if k % 2 else keep_ref
        start = pl.multiple_of((me ^ k) * tile, tile)
        out_ref[k // 2] = cot_ref[:, pl.ds(start, tile)]


def live_loop(count, products, add):
    def group(g, carry):
        first = g * UNROLL
        found = [products(first + u) for u in range(UNROLL)]
        for u in range(UNROLL):
            add(first + u, jnp.where(first + u < count, found[u], 0.0))
        return carry

    lax.fori_loop(0, (count + UNROLL - 1) // UNROLL, group, 0)


def aggregate_kernel(row_turn, col_order, meta, x_ref, vals_ref, out_ref, acc):
    listed, tile = vals_ref.shape[:2]
    per = x_ref.shape[2] // tile
    acc[...] = jnp.zeros_like(acc)

    def product(t):
        at = meta[listed + t]
        start = pl.multiple_of((at % per) * tile, tile)
        return lax.dot_general(
            x_ref[(at // per + x_ref.shape[0] - row_turn) % x_ref.shape[0], :, pl.ds(start, tile)],
            vals_ref[t],
            (((1,), (1,)), ((), ())),
            preferred_element_type=F32,
        )

    def add(t, found):
        acc[meta[t]] = acc[meta[t]] + found

    live_loop(meta[2 * listed], product, add)
    for i, c in enumerate(col_order):
        out_ref[i * per : (i + 1) * per] = acc[c * per : (c + 1) * per].astype(out_ref.dtype)


def tile_kernel(part_ref, w_ref, low_ref, high_ref, out_ref, cot_all):
    groups, _, tile = out_ref.shape
    feat = part_ref.shape[1]
    half, outs = low_ref.shape[:2]
    me = lax.axis_index("rep")
    for k in range(groups):
        cot_all[me ^ k] = low_ref[k] if k < half else high_ref[k - half]
    h = jnp.sum(
        part_ref[...].reshape(-1, groups * feat, tile).astype(F32), axis=0
    ).astype(BF16)
    w = w_ref[...]
    pre = lax.dot_general(w, h, (((0,), (0,)), ((), ())), preferred_element_type=F32)
    sig = jax.nn.sigmoid(pre)
    cot = cot_all[...].reshape(groups * outs, tile).astype(F32)
    dpre = (cot * sig * (1.0 + pre * (1.0 - sig))).astype(BF16)
    dagg = jnp.dot(w, dpre, preferred_element_type=F32)
    grad = lax.dot_general(dpre, h, (((1,), (1,)), ((), ())), preferred_element_type=F32)
    y = pre * sig
    dtype = out_ref.dtype
    out_ref[:, :feat] = dagg.astype(dtype).reshape(groups, feat, tile)
    out_ref[:, feat : feat + outs] = y.astype(dtype).reshape(groups, outs, tile)
    high = grad.astype(dtype)
    low = (grad - high.astype(F32)).astype(dtype)
    out_ref[:, feat + outs : feat + 2 * outs] = high.reshape(groups, outs, tile)
    out_ref[:, feat + 2 * outs :] = low.reshape(groups, outs, tile)


def pack_kernel(in_ref, out_ref):
    tiles, in_rows, tile = in_ref.shape
    outs = (in_rows * tiles - out_ref.shape[1]) // (3 * tiles - 1)
    feat = in_rows - 3 * outs
    rows = tiles * feat
    dagg = in_ref[:, :feat].reshape(rows, tile)
    grad = jnp.sum(in_ref[:, feat + outs :].astype(F32), axis=0)
    grad = (grad[:outs] + grad[outs:]).astype(out_ref.dtype)
    for i in range(out_ref.shape[0]):
        out_ref[i, :rows] = dagg
        out_ref[i, rows:] = grad


def backward_kernel(row_turn, col_order, meta, d_ref, vals_ref, out_ref, acc):
    listed = vals_ref.shape[0]
    parts, rows, tile = out_ref.shape
    per = acc.shape[0] // parts
    feat = acc.shape[1]
    slab_rows = per * feat
    acc[...] = jnp.zeros_like(acc)

    def product(t):
        at = meta[t]
        start = pl.multiple_of((at % per) * feat, feat)
        return jnp.dot(
            d_ref[place_of(at // per, col_order), pl.ds(start, feat), :],
            vals_ref[t],
            preferred_element_type=F32,
        )

    def add(t, found):
        at = meta[listed + t]
        acc[at] = acc[at] + found

    live_loop(meta[2 * listed], product, add)
    grad = jnp.sum(d_ref[:, slab_rows:, :].astype(F32), axis=0).astype(out_ref.dtype)
    for i in range(parts):
        r = (i + row_turn) % parts
        out_ref[i, :slab_rows] = (
            acc[r * per : (r + 1) * per].reshape(slab_rows, tile).astype(out_ref.dtype)
        )
        out_ref[i, slab_rows:] = grad


def final_kernel(in_ref, mid_ref, dx_ref, y_ref, grad_ref):
    feat = dx_ref.shape[0]
    tile = in_ref.shape[2]
    slab_rows = in_ref.shape[1] - grad_ref.shape[0]
    for i in range(slab_rows // feat):
        dx_ref[:, i * tile : (i + 1) * tile] = jnp.sum(
            in_ref[:, i * feat : (i + 1) * feat, :].astype(F32), axis=0
        )
    grad_ref[...] = jnp.sum(in_ref[:, slab_rows:, :].astype(F32), axis=0)
    outs = y_ref.shape[0]
    for i in range(mid_ref.shape[0]):
        y_ref[:, i * tile : (i + 1) * tile] = mid_ref[i, feat : feat + outs]


def place_of(member, order):
    place = jnp.int32(0)
    for i, listed in enumerate(order):
        if i > 0:
            place = jnp.where(member == listed, i, place)
    return place


def exchange(parts, axis, order=None):
    groups = None if order is None else [list(order)]
    return lax.all_to_all(parts, axis, 0, 0, axis_index_groups=groups, tiled=True)


def swap(parts, bit):
    n = lax.axis_size("rep")
    return lax.ppermute(parts, "rep", [(i, i ^ bit) for i in range(n)])


def local(x_t, weight, cotangent_t, tile_vals, tile_rows, tile_cols, tile_count):
    feat, slab = x_t.shape
    tile = tile_vals.shape[-1]
    listed = tile_vals.shape[2]
    per = slab // tile
    n_row, n_col, n_rep = lax.axis_size("row"), lax.axis_size("col"), lax.axis_size("rep")
    out_loc = weight.shape[1] // n_rep
    row_turn, col_turn = n_row // 4, n_col // 2
    row_order = [(i + row_turn) % n_row for i in range(n_row)]
    col_order = sorted(range(n_col), key=lambda c: (c != col_turn, c != 0, -c))
    grad_shape = (out_loc, n_rep * feat)
    shape = jax.ShapeDtypeStruct

    meta = jnp.concatenate([tile_rows[0, 0], tile_cols[0, 0], tile_count[0]])

    x_parts = call(copies_kernel, shape((n_row, feat, slab), BF16), [VMEM], "copies")(x_t)
    x_all = exchange(x_parts, "row", row_order)
    half = shape((n_rep // 2, out_loc, tile), BF16)
    keep, send = call(cut_kernel, (half, half), [VMEM], "cut")(cotangent_t)
    got = swap(send, 1)
    keep, send = (
        jnp.stack([keep[i], got[i], keep[i + 2], got[i + 2]]) for i in range(2)
    )
    got = swap(send, 2)
    keep, send = (
        jnp.stack([keep[i], keep[i + 1], got[i], got[i + 1]]) for i in (0, 2)
    )
    x_all, keep, send = lax.optimization_barrier((x_all, keep, send))
    got = swap(send, 4)
    vals = call(
        stage_kernel,
        shape((listed, tile, tile), BF16),
        [HBM],
        "stage",
        [pltpu.SemaphoreType.DMA((8,))],
    )(tile_vals[0, 0])

    part = call(
        functools.partial(aggregate_kernel, row_turn, col_order),
        shape((n_col * per, feat, tile), BF16),
        [SMEM, VMEM, VMEM],
        "aggregate",
        [pltpu.VMEM((n_col * per, feat, tile), F32)],
    )(meta, x_all, vals)
    order = [c * n_rep + i for c in col_order for i in range(n_rep)]
    part = exchange(part, ("col", "rep"), order)

    mid_rows = feat + 3 * out_loc
    mid = call(
        tile_kernel,
        shape((n_rep, mid_rows, tile), BF16),
        [VMEM] * 4,
        "tile",
        [pltpu.VMEM((n_rep, out_loc, tile), BF16)],
    )(part, weight, keep, got)
    mid = exchange(mid, "rep")
    send = call(pack_kernel, shape((n_col, per * feat + out_loc, tile), BF16), [VMEM], "pack")(mid)
    d_all = exchange(send, "col", col_order)

    back = call(
        functools.partial(backward_kernel, row_turn, col_order),
        shape((n_row, per * feat + out_loc, tile), BF16),
        [SMEM, VMEM, VMEM],
        "backward",
        [pltpu.VMEM((n_row * per, feat, tile), F32)],
    )(meta, d_all, vals)
    back = exchange(back, "row", row_order)

    dx, y, grad = call(
        final_kernel,
        (shape((feat, slab), F32), shape((out_loc, slab), BF16), shape(grad_shape, F32)),
        [VMEM, VMEM],
        "final",
    )(back, mid)
    return y, dx, grad.T


def solution(mesh):
    return jax.shard_map(
        local,
        mesh=mesh,
        in_specs=(
            P("rep", ("row", "col")),
            P(),
            P("rep", ("row", "col")),
            P("row", "col", None, None, None),
            P("row", "col", None),
            P("row", "col", None),
            P("row", "col"),
        ),
        out_specs=(P("rep", ("row", "col")), P("rep", ("row", "col")), P(None, "rep")),
        check_vma=False,
    )
```

```python
import functools

import jax
import jax.numpy as jnp
from jax import lax
from jax.experimental import pallas as pl
from jax.experimental.pallas import tpu as pltpu
from jax.sharding import PartitionSpec as P

BF16 = jnp.bfloat16
F32 = jnp.float32
UNROLL = 32
SMEM = pl.BlockSpec(memory_space=pltpu.SMEM)
VMEM = pl.BlockSpec(memory_space=pltpu.VMEM)
HBM = pl.BlockSpec(memory_space=pltpu.HBM)
PARAMS = pltpu.CompilerParams(vmem_limit_bytes=24 * 1024 * 1024)


def call(kernel, out, in_specs, name, scratch=()):
    return pl.pallas_call(
        kernel,
        out_shape=out,
        in_specs=in_specs,
        out_specs=jax.tree.map(lambda _: VMEM, out),
        scratch_shapes=list(scratch),
        compiler_params=PARAMS,
        name=name,
    )


def copies_kernel(x_ref, out_ref):
    for r in range(out_ref.shape[0]):
        out_ref[r] = x_ref[...]


def stage_kernel(vals_hbm, vals_ref, sems):
    n = sems.shape[0]
    per = vals_ref.shape[0] // n
    copies = [
        pltpu.make_async_copy(
            vals_hbm.at[pl.ds(i * per, per)], vals_ref.at[pl.ds(i * per, per)], sems.at[i]
        )
        for i in range(n)
    ]
    for copy in copies:
        copy.start()
    for copy in copies:
        copy.wait()


def cut_kernel(cot_ref, keep_ref, send_ref):
    tile = keep_ref.shape[2]
    me = lax.axis_index("rep")
    for k in range(2 * keep_ref.shape[0]):
        out_ref = send_ref if k % 2 else keep_ref
        start = pl.multiple_of((me ^ k) * tile, tile)
        out_ref[k // 2] = cot_ref[:, pl.ds(start, tile)]


def live_loop(count, products, add):
    def group(g, carry):
        first = g * UNROLL
        found = [products(first + u) for u in range(UNROLL)]
        for u in range(UNROLL):
            add(first + u, jnp.where(first + u < count, found[u], 0.0))
        return carry

    lax.fori_loop(0, (count + UNROLL - 1) // UNROLL, group, 0)


def aggregate_kernel(row_turn, col_order, meta, x_ref, vals_ref, out_ref, acc):
    listed, tile = vals_ref.shape[:2]
    per = x_ref.shape[2] // tile
    acc[...] = jnp.zeros_like(acc)

    def product(t):
        at = meta[listed + t]
        start = pl.multiple_of((at % per) * tile, tile)
        return lax.dot_general(
            x_ref[(at // per + x_ref.shape[0] - row_turn) % x_ref.shape[0], :, pl.ds(start, tile)],
            vals_ref[t],
            (((1,), (1,)), ((), ())),
            preferred_element_type=F32,
        )

    def add(t, found):
        acc[meta[t]] = acc[meta[t]] + found

    live_loop(meta[2 * listed], product, add)
    for i, c in enumerate(col_order):
        out_ref[i * per : (i + 1) * per] = acc[c * per : (c + 1) * per].astype(out_ref.dtype)


def tile_kernel(part_ref, w_ref, low_ref, high_ref, out_ref, cot_all):
    groups, _, tile = out_ref.shape
    feat = part_ref.shape[1]
    half, outs = low_ref.shape[:2]
    me = lax.axis_index("rep")
    for k in range(groups):
        cot_all[me ^ k] = low_ref[k] if k < half else high_ref[k - half]
    h = jnp.sum(
        part_ref[...].reshape(-1, groups * feat, tile).astype(F32), axis=0
    ).astype(BF16)
    w = w_ref[...]
    pre = lax.dot_general(w, h, (((0,), (0,)), ((), ())), preferred_element_type=F32)
    sig = jax.nn.sigmoid(pre)
    cot = cot_all[...].reshape(groups * outs, tile).astype(F32)
    dpre = (cot * sig * (1.0 + pre * (1.0 - sig))).astype(BF16)
    dagg = jnp.dot(w, dpre, preferred_element_type=F32)
    grad = lax.dot_general(dpre, h, (((1,), (1,)), ((), ())), preferred_element_type=F32)
    y = pre * sig
    dtype = out_ref.dtype
    out_ref[:, :feat] = dagg.astype(dtype).reshape(groups, feat, tile)
    out_ref[:, feat : feat + outs] = y.astype(dtype).reshape(groups, outs, tile)
    high = grad.astype(dtype)
    low = (grad - high.astype(F32)).astype(dtype)
    out_ref[:, feat + outs : feat + 2 * outs] = high.reshape(groups, outs, tile)
    out_ref[:, feat + 2 * outs :] = low.reshape(groups, outs, tile)


def pack_kernel(in_ref, out_ref):
    tiles, in_rows, tile = in_ref.shape
    outs = (in_rows * tiles - out_ref.shape[1]) // (3 * tiles - 1)
    feat = in_rows - 3 * outs
    rows = tiles * feat
    dagg = in_ref[:, :feat].reshape(rows, tile)
    grad = jnp.sum(in_ref[:, feat + outs :].astype(F32), axis=0)
    grad = (grad[:outs] + grad[outs:]).astype(out_ref.dtype)
    for i in range(out_ref.shape[0]):
        out_ref[i, :rows] = dagg
        out_ref[i, rows:] = grad


def backward_kernel(grad_rows, col_order, meta, d_ref, vals_ref, out_ref, acc):
    listed = vals_ref.shape[0]
    inner, rows, tile = out_ref.shape
    feat = acc.shape[1]
    slab_rows = d_ref.shape[1] - grad_rows
    per = slab_rows // feat
    outer = rows // slab_rows
    acc[...] = jnp.zeros_like(acc)

    def product(t):
        at = meta[t]
        start = pl.multiple_of((at % per) * feat, feat)
        return jnp.dot(
            d_ref[place_of(at // per, col_order), pl.ds(start, feat), :],
            vals_ref[t],
            preferred_element_type=F32,
        )

    def add(t, found):
        at = meta[listed + t]
        acc[at] = acc[at] + found

    live_loop(meta[2 * listed], product, add)
    grad = jnp.sum(d_ref[:, slab_rows:, :].astype(F32), axis=0).astype(out_ref.dtype)
    for i in range(inner):
        for o in range(outer):
            first = (o * inner + i) * per
            out_ref[i, o * slab_rows : (o + 1) * slab_rows] = (
                acc[first : first + per].reshape(slab_rows, tile).astype(out_ref.dtype)
            )
        out_ref[i, outer * slab_rows :] = grad


def fold_kernel(turn, in_ref, out_ref):
    outer, rows, _ = out_ref.shape
    total = jnp.sum(in_ref[...].astype(F32), axis=0).astype(out_ref.dtype)
    slab_rows = (total.shape[0] - rows) // (outer - 1)
    for i in range(outer):
        o = (i + turn) % outer
        out_ref[i, :slab_rows] = total[o * slab_rows : (o + 1) * slab_rows]
        out_ref[i, slab_rows:] = total[outer * slab_rows :]


def final_kernel(in_ref, mid_ref, dx_ref, y_ref, grad_ref):
    feat = dx_ref.shape[0]
    tile = in_ref.shape[2]
    slab_rows = in_ref.shape[1] - grad_ref.shape[0]
    for i in range(slab_rows // feat):
        dx_ref[:, i * tile : (i + 1) * tile] = jnp.sum(
            in_ref[:, i * feat : (i + 1) * feat, :].astype(F32), axis=0
        )
    grad_ref[...] = jnp.sum(in_ref[:, slab_rows:, :].astype(F32), axis=0)
    outs = y_ref.shape[0]
    for i in range(mid_ref.shape[0]):
        y_ref[:, i * tile : (i + 1) * tile] = mid_ref[i, feat : feat + outs]


def place_of(member, order):
    place = jnp.int32(0)
    for i, listed in enumerate(order):
        if i > 0:
            place = jnp.where(member == listed, i, place)
    return place


def exchange(parts, axis, order=None):
    groups = None if order is None else [list(order)]
    return lax.all_to_all(parts, axis, 0, 0, axis_index_groups=groups, tiled=True)


def swap(parts, bit):
    n = lax.axis_size("rep")
    return lax.ppermute(parts, "rep", [(i, i ^ bit) for i in range(n)])


def local(x_t, weight, cotangent_t, tile_vals, tile_rows, tile_cols, tile_count):
    feat, slab = x_t.shape
    tile = tile_vals.shape[-1]
    listed = tile_vals.shape[2]
    per = slab // tile
    n_row, n_col, n_rep = lax.axis_size("row"), lax.axis_size("col"), lax.axis_size("rep")
    out_loc = weight.shape[1] // n_rep
    row_turn, col_turn = n_row // 4, n_col // 2
    row_order = [(i + row_turn) % n_row for i in range(n_row)]
    col_order = sorted(range(n_col), key=lambda c: (c != col_turn, c != 0, -c))
    inner = 4 if n_row % 4 == 0 else 1
    outer = n_row // inner
    outer_turn = outer // 4
    inner_groups = [[o * inner + i for i in range(inner)] for o in range(outer)]
    outer_groups = [
        [(o + outer_turn) % outer * inner + i for o in range(outer)] for i in range(inner)
    ]
    grad_shape = (out_loc, n_rep * feat)
    shape = jax.ShapeDtypeStruct

    meta = jnp.concatenate([tile_rows[0, 0], tile_cols[0, 0], tile_count[0]])

    x_parts = call(copies_kernel, shape((n_row, feat, slab), BF16), [VMEM], "copies")(x_t)
    x_all = exchange(x_parts, "row", row_order)
    half = shape((n_rep // 2, out_loc, tile), BF16)
    keep, send = call(cut_kernel, (half, half), [VMEM], "cut")(cotangent_t)
    got = swap(send, 1)
    keep, send = (
        jnp.stack([keep[i], got[i], keep[i + 2], got[i + 2]]) for i in range(2)
    )
    got = swap(send, 2)
    keep, send = (
        jnp.stack([keep[i], keep[i + 1], got[i], got[i + 1]]) for i in (0, 2)
    )
    x_all, keep, send = lax.optimization_barrier((x_all, keep, send))
    got = swap(send, 4)
    vals = call(
        stage_kernel,
        shape((listed, tile, tile), BF16),
        [HBM],
        "stage",
        [pltpu.SemaphoreType.DMA((8,))],
    )(tile_vals[0, 0])

    part = call(
        functools.partial(aggregate_kernel, row_turn, col_order),
        shape((n_col * per, feat, tile), BF16),
        [SMEM, VMEM, VMEM],
        "aggregate",
        [pltpu.VMEM((n_col * per, feat, tile), F32)],
    )(meta, x_all, vals)
    order = [c * n_rep + i for c in col_order for i in range(n_rep)]
    part = exchange(part, ("col", "rep"), order)

    mid_rows = feat + 3 * out_loc
    mid = call(
        tile_kernel,
        shape((n_rep, mid_rows, tile), BF16),
        [VMEM] * 4,
        "tile",
        [pltpu.VMEM((n_rep, out_loc, tile), BF16)],
    )(part, weight, keep, got)
    mid = exchange(mid, "rep")
    send = call(pack_kernel, shape((n_col, per * feat + out_loc, tile), BF16), [VMEM], "pack")(mid)
    d_all = exchange(send, "col", col_order)

    back = call(
        functools.partial(backward_kernel, out_loc, col_order),
        shape((inner, outer * per * feat + out_loc, tile), BF16),
        [SMEM, VMEM, VMEM],
        "backward",
        [pltpu.VMEM((n_row * per, feat, tile), F32)],
    )(meta, d_all, vals)
    back = lax.all_to_all(back, "row", 0, 0, axis_index_groups=inner_groups, tiled=True)
    back = call(
        functools.partial(fold_kernel, outer_turn),
        shape((outer, per * feat + out_loc, tile), BF16),
        [VMEM],
        "fold",
    )(back)
    back = lax.all_to_all(back, "row", 0, 0, axis_index_groups=outer_groups, tiled=True)

    dx, y, grad = call(
        final_kernel,
        (shape((feat, slab), F32), shape((out_loc, slab), BF16), shape(grad_shape, F32)),
        [VMEM, VMEM],
        "final",
    )(back, mid)
    return y, dx, grad.T


def solution(mesh):
    return jax.shard_map(
        local,
        mesh=mesh,
        in_specs=(
            P("rep", ("row", "col")),
            P(),
            P("rep", ("row", "col")),
            P("row", "col", None, None, None),
            P("row", "col", None),
            P("row", "col", None),
            P("row", "col"),
        ),
        out_specs=(P("rep", ("row", "col")), P("rep", ("row", "col")), P(None, "rep")),
        check_vma=False,
    )
```
